256 devices in a mesh: samp: 32 (over z, y_lo, core), par: 8 (over y_hi, x).
Axes of the slice: x: 4, y: 4 (y_hi: 2, y_lo: 2; y = y_hi * 2 + y_lo), z: 8, core: 2. Of those that a mesh axis runs over, the one named last changes fastest.
Arguments:
- jacobian: float32 [8192, 8192], P('samp', 'par'), may hold values from -60 to 60, as said below
Outputs:
- gram: float32 [8192, 8192], P('samp', 'par')
The draws below stay inside these ranges and needn't reach their ends.
Inputs may be any that keep to these rules, and one draw needn't show every extreme that they name: `jacobian`: real-valued log-derivatives.
All inputs are finite; a program needn't handle non-finite values.
Results may differ from the reference program's by a relative error of at most 0.000065.
Values sent between devices are 32-bit elements; how exact they have to be, the bound alone decides.
No kernel may reach another device: no remote copies, remote signals or barrier semaphores. Data moves between devices by JAX's collectives and lax.ppermute only.
A program may use at most 128 MiB of HBM per device.

```python
import jax
import jax.numpy as jnp
from jax import lax

P_SIZE = 8192
SAMPLES = 8192


def draw_jacobian(key, part):
    key = jax.random.fold_in(key, 7)
    k_rough, k_col, k_row, k_off = jax.random.split(key, 4)
    col_scale = jnp.exp(jax.random.uniform(k_col, (P_SIZE,), jnp.float32, jnp.log(0.3), jnp.log(3.0)))
    offset = jax.random.normal(k_off, (P_SIZE,), jnp.float32)
    ramp = 0.5 + jnp.arange(SAMPLES, dtype=jnp.float32) / SAMPLES
    rough = jax.random.normal(k_rough, (SAMPLES, P_SIZE), jnp.float32)
    row_scale = jnp.exp(jax.random.uniform(k_row, (SAMPLES,), jnp.float32, jnp.log(0.5), jnp.log(2.0)))
    rough = jnp.clip(rough, -6.0, 6.0)
    return row_scale[:, None] * col_scale[None, :] * rough + offset[None, :] * ramp[:, None]


def setup_inputs(seed: int = 0) -> dict:
    arg_keys = jax.random.split(jax.random.key(seed), 2)
    return {
        "jacobian": draw_jacobian(jax.random.fold_in(arg_keys[1], 71), 0),
    }


def reference(jacobian):
    mean = jnp.sum(jacobian, axis=0) / SAMPLES
    centred = jacobian - mean[None, :]
    product = jnp.dot(centred, centred.T, preferred_element_type=jnp.float32, precision=lax.Precision.HIGHEST)
    return product / SAMPLES
```

```python
import jax
import jax.numpy as jnp
from jax import lax
from jax.sharding import PartitionSpec as P

AXES = ("samp", "par")
Z, S, YH, X = 8, 4, 2, 4


def number(z, s, yh, x):
    return ((z % Z) * S + s) * YH * X + yh * X + x % X


def pairs(place, keep=lambda z, s, yh, x: True):
    return [
        (number(z, s, yh, x), number(*place(z, s, yh, x)))
        for z in range(Z)
        for s in range(S)
        for yh in range(YH)
        for x in range(X)
        if keep(z, s, yh, x)
    ]


def move(value, place, keep=lambda z, s, yh, x: True):
    return lax.ppermute(value, AXES, pairs(place, keep))


def along_z(step):
    return lambda z, s, yh, x: (z + step, s, yh, x)


def along_x(step):
    return lambda z, s, yh, x: (z, s, yh, x + step)


def flip_s(bits):
    return lambda z, s, yh, x: (z, s ^ bits, yh, x)


def flip_z(bits):
    return lambda z, s, yh, x: (z ^ bits, s, yh, x)


def other_yh(z, s, yh, x):
    return (z, s, 1 - yh, x)


def product(left, right):
    return lax.dot_general(
        left,
        right,
        (((1,), (1,)), ((), ())),
        precision=lax.Precision.HIGH,
        preferred_element_type=jnp.float32,
    )


GROUPS = ((0, 1, 7), (2, 6), (3, 5), (4,))


def per_device(jacobian):
    rows = jacobian.shape[0]
    half = rows // 2
    samples = rows * Z * S
    samp, par = lax.axis_index("samp"), lax.axis_index("par")
    z, s, yh, x = samp // S, samp % S, par // X, par % X

    near = move(jacobian, flip_s(2))
    total = jnp.sum(jacobian, axis=0, keepdims=True)
    for place in (flip_z(1), flip_z(2), flip_z(4)):
        total = total + move(total, place)
    shift = total / (rows * Z)

    shifted = jacobian - shift
    up, down = [shifted], [shifted]
    for step in range(1, Z // 2):
        up.append(move(up[-1], along_z(1)))
        down.append(move(down[-1], along_z(-1)))
    far = (move(up[-1][:half], along_z(1)), move(down[-1][half:], along_z(-1)))

    for place in (flip_s(2), flip_s(1)):
        total = total + move(total, place)
    mean = total / samples
    rest = shift - mean

    pair = jnp.stack([jacobian, near])
    pair = jnp.concatenate([pair[:, None], move(pair, flip_s(1))[:, None]], axis=1)
    pair = pair.reshape(S, rows, jacobian.shape[1])
    left = [
        lax.dynamic_index_in_dim(pair, ((x + k) % X) ^ s, 0, keepdims=False) - mean
        for k in range(X)
    ]

    blocks = {0: shifted, 4: jnp.concatenate(far, axis=0)}
    for step in range(1, Z // 2):
        blocks[Z - step] = up[step]
        blocks[step] = down[step]

    done = {}
    for group in GROUPS:
        right = [blocks[step] + rest for step in group]

        def piece(k):
            return jnp.stack([product(left[k], block) for block in right])

        across = piece(2)
        got_up = move(across[:, :half], along_x(1))
        got_down = move(across[:, half:], along_x(-1))
        above, below = piece(1), piece(3)
        above = jnp.concatenate([above[:, :half] + got_up, above[:, half:]], axis=1)
        below = jnp.concatenate([below[:, :half], below[:, half:] + got_down], axis=1)
        part = piece(0) + move(above, along_x(1)) + move(below, along_x(-1))
        part = part + move(part, other_yh)
        for i, step in enumerate(group):
            done[step] = part[i]
    done = jnp.stack([done[step] for step in range(Z)])

    got = []
    for turn in range(X):
        step = (X * yh + (s + turn) % X - z) % Z
        block = lax.dynamic_index_in_dim(done, step, 0, keepdims=False)
        got.append(move(block, lambda z, s, yh, x: (z, x, yh, s + turn)))
    got = jnp.stack(got)
    out = [
        lax.dynamic_index_in_dim(got, (x - m) % X, 0, keepdims=False) for m in range(X)
    ]
    return jnp.concatenate(out, axis=1) / samples


def solution(mesh):
    placed = (P("samp", "par"),)
    return jax.shard_map(
        per_device, mesh=mesh, in_specs=placed, out_specs=P("samp", "par"), check_vma=False
    )
```

```python
import jax
import jax.numpy as jnp
from jax import lax
from jax.sharding import PartitionSpec as P

AXES = ("samp", "par")
Z, S, YH, X = 8, 4, 2, 4


def number(z, s, yh, x):
    return ((z % Z) * S + s) * YH * X + yh * X + x % X


def pairs(place, keep=lambda z, s, yh, x: True):
    return [
        (number(z, s, yh, x), number(*place(z, s, yh, x)))
        for z in range(Z)
        for s in range(S)
        for yh in range(YH)
        for x in range(X)
        if keep(z, s, yh, x)
    ]


def move(value, place, keep=lambda z, s, yh, x: True):
    return lax.ppermute(value, AXES, pairs(place, keep))


def along_z(step):
    return lambda z, s, yh, x: (z + step, s, yh, x)


def flip_s(bits):
    return lambda z, s, yh, x: (z, s ^ bits, yh, x)


def first_x(z, s, yh, x):
    return (z, s, yh, x ^ (3 if s % 2 else 1))


def second_x(z, s, yh, x):
    return (z, s, yh, x ^ (1 if s % 2 else 3))


def other_yh(z, s, yh, x):
    return (z, s, 1 - yh, x)


def product(left, right):
    return lax.dot_general(
        left,
        right,
        (((1,), (1,)), ((), ())),
        precision=lax.Precision.HIGH,
        preferred_element_type=jnp.float32,
    )


def pin(value, token):
    corner = value[:8, :128] + 0.0 * token.reshape(-1, token.shape[-1])[:8, :128]
    return lax.dynamic_update_slice(value, corner, (0, 0))


def both(up, down):
    return move(up, along_z(1)), move(down, along_z(-1))


def per_device(jacobian):
    rows = jacobian.shape[0]
    half = rows // 2
    samples = rows * Z * S
    samp, par = lax.axis_index("samp"), lax.axis_index("par")
    z, s, yh, x = samp // S, samp % S, par // X, par % X

    one = both(jacobian, jacobian)
    near = move(jacobian, flip_s(2))
    core = move(jacobian, flip_s(1))

    total = jnp.sum(jacobian, axis=0, keepdims=True)
    totals = jnp.broadcast_to(total, (Z * S, total.shape[1]))
    totals = lax.all_to_all(totals, "samp", 0, 0, tiled=True)
    mean = jnp.sum(totals, axis=0, keepdims=True) / samples

    two = both(*one)
    near = near - mean
    near_core = move(near, flip_s(1))
    plane = jnp.stack([jacobian - mean, core - mean, near, near_core])
    second = jnp.where(s % 2 == 0, x ^ 3, x ^ 1)
    left = [
        lax.dynamic_index_in_dim(plane, place ^ s, 0, keepdims=False)
        for place in (x, second, second ^ 2, x ^ 2)
    ]

    def products(blocks, places):
        return jnp.stack(
            [jnp.concatenate([product(left[k], b) for k in places], axis=0) for b in blocks]
        )

    def halve_x(blocks):
        got = move(products(blocks, (2, 3)), first_x)
        return got, products(blocks, (0, 1))

    def quarter_x(got, kept):
        kept = kept + got
        return kept[:, :rows], move(kept[:, rows:], second_x)

    got1, kept1 = halve_x([b - mean for b in (jacobian, *one)])
    own1, got1 = quarter_x(got1, kept1)

    two = [pin(b, kept1) for b in two]
    three = both(*two)
    got2, kept2 = halve_x([b - mean for b in two])
    part1 = own1 + got1
    part1 = part1 + move(part1, other_yh)
    own2, got2 = quarter_x(got2, kept2)

    three = [pin(b, kept2) for b in three]
    far = both(three[0][:half], three[1][half:])
    got3, kept3 = halve_x([b - mean for b in three])
    part2 = own2 + got2
    part2 = part2 + move(part2, other_yh)
    own3, got3 = quarter_x(got3, kept3)

    far = jnp.concatenate([pin(far[0], kept3), far[1]], axis=0)
    got4, kept4 = halve_x([far - mean])
    part3 = own3 + got3
    part3 = part3 + move(part3, other_yh)
    own4, got4 = quarter_x(got4, kept4)
    part4 = own4 + got4
    part4 = part4 + move(part4, other_yh)

    done = jnp.stack(
        [part1[0], part1[2], part2[1], part3[1], part4[0], part3[0], part2[0], part1[1]]
    )

    got = []
    for turn in range(X):
        step = (X * yh + (s + turn) % X - z) % Z
        block = lax.dynamic_index_in_dim(done, step, 0, keepdims=False)
        got.append(move(block, lambda z, s, yh, x: (z, x, yh, s + turn)))
    got = jnp.stack(got)
    out = [
        lax.dynamic_index_in_dim(got, (x - m) % X, 0, keepdims=False) for m in range(X)
    ]
    return jnp.concatenate(out, axis=1) / samples


def solution(mesh):
    placed = (P("samp", "par"),)
    return jax.shard_map(
        per_device, mesh=mesh, in_specs=placed, out_specs=P("samp", "par"), check_vma=False
    )
```

```python
import jax
import jax.numpy as jnp
from jax import lax
from jax.sharding import PartitionSpec as P

AXES = ("samp", "par")
Z, S, YH, X = 8, 4, 2, 4


def number(z, s, yh, x):
    return ((z % Z) * S + s) * YH * X + yh * X + x % X


def pairs(place, keep=lambda z, s, yh, x: True):
    return [
        (number(z, s, yh, x), number(*place(z, s, yh, x)))
        for z in range(Z)
        for s in range(S)
        for yh in range(YH)
        for x in range(X)
        if keep(z, s, yh, x)
    ]


def move(value, place, keep=lambda z, s, yh, x: True):
    return lax.ppermute(value, AXES, pairs(place, keep))


def along_z(step):
    return lambda z, s, yh, x: (z + step, s, yh, x)


def flip_s(bits):
    return lambda z, s, yh, x: (z, s ^ bits, yh, x)


def first_x(z, s, yh, x):
    return (z, s, yh, x ^ (3 if s % 2 else 1))


def second_x(z, s, yh, x):
    return (z, s, yh, x ^ (1 if s % 2 else 3))


def other_yh(z, s, yh, x):
    return (z, s, 1 - yh, x)


def product(left, right):
    return lax.dot_general(
        left,
        right,
        (((1,), (1,)), ((), ())),
        precision=lax.Precision.HIGH,
        preferred_element_type=jnp.float32,
    )


def pin(value, token):
    corner = value[:8, :128] + 0.0 * token.reshape(-1, token.shape[-1])[:8, :128]
    return lax.dynamic_update_slice(value, corner, (0, 0))


def tie(value, token):
    return value + 0.0 * token[(0,) * token.ndim]


def both(up, down):
    return move(up, along_z(1)), move(down, along_z(-1))


def per_device(jacobian):
    rows = jacobian.shape[0]
    half = rows // 2
    samples = rows * Z * S
    samp, par = lax.axis_index("samp"), lax.axis_index("par")
    z, s, yh, x = samp // S, samp % S, par // X, par % X

    one = both(jacobian, jacobian)
    near = move(jacobian, flip_s(2))
    core = move(jacobian, flip_s(1))

    total = jnp.sum(jacobian, axis=0, keepdims=True)
    totals = jnp.broadcast_to(total, (Z * S, total.shape[1]))
    totals = lax.all_to_all(totals, "samp", 0, 0, tiled=True)
    mean = jnp.sum(totals, axis=0, keepdims=True) / samples

    two = both(*one)
    near = pin(near, one[0][:8] + one[1][:8]) - mean
    near_core = move(near, flip_s(1))
    plane = jnp.stack([jacobian - mean, core - mean, near, near_core])
    second = jnp.where(s % 2 == 0, x ^ 3, x ^ 1)
    left = [
        lax.dynamic_index_in_dim(plane, place ^ s, 0, keepdims=False)
        for place in (x, second, second ^ 2, x ^ 2)
    ]

    def products(blocks, places):
        return jnp.stack(
            [jnp.concatenate([product(left[k], b) for k in places], axis=0) for b in blocks]
        )

    def halve_x(blocks, token=None):
        got = move(products([b - mean for b in blocks], (2, 3)), first_x)
        centre = mean if token is None else tie(mean, token)
        return got, products([b - centre for b in blocks], (0, 1))

    def quarter_x(got, kept):
        kept = kept + got
        return kept[:, :rows], move(kept[:, rows:], second_x)

    got1, kept1 = halve_x((jacobian, *one))
    own1, got1 = quarter_x(got1, kept1)

    two = [pin(b, kept1) for b in two]
    three = both(*two)
    part1 = own1 + got1
    got2, kept2 = halve_x(two, part1)
    part1 = part1 + move(part1, other_yh)
    own2, got2 = quarter_x(got2, kept2)

    three = [pin(b, kept2) for b in three]
    far = both(three[0][:half], three[1][half:])
    part2 = own2 + got2
    got3, kept3 = halve_x(three, None)
    part2 = part2 + move(part2, other_yh)
    own3, got3 = quarter_x(got3, kept3)

    far = jnp.concatenate([far[0], far[1]], axis=0)
    part3 = own3 + got3
    got4, kept4 = halve_x([far], None)
    part3 = part3 + move(part3, other_yh)
    own4, got4 = quarter_x(got4, kept4)
    part4 = own4 + got4
    part4 = part4 + move(part4, other_yh)

    done = jnp.stack(
        [part1[0], part1[2], part2[1], part3[1], part4[0], part3[0], part2[0], part1[1]]
    )

    got = []
    for turn in range(X):
        step = (X * yh + (s + turn) % X - z) % Z
        block = lax.dynamic_index_in_dim(done, step, 0, keepdims=False)
        got.append(move(block, lambda z, s, yh, x: (z, x, yh, s + turn)))
    got = jnp.stack(got)
    out = [
        lax.dynamic_index_in_dim(got, (x - m) % X, 0, keepdims=False) for m in range(X)
    ]
    return jnp.concatenate(out, axis=1) / samples


def solution(mesh):
    placed = (P("samp", "par"),)
    return jax.shard_map(
        per_device, mesh=mesh, in_specs=placed, out_specs=P("samp", "par"), check_vma=False
    )
```

```python
import jax
import jax.numpy as jnp
from jax import lax
from jax.sharding import PartitionSpec as P

AXES = ("samp", "par")
Z, S, YH, X = 8, 4, 2, 4


def number(z, s, yh, x):
    return ((z % Z) * S + s) * YH * X + yh * X + x % X


def pairs(place, keep=lambda z, s, yh, x: True):
    return [
        (number(z, s, yh, x), number(*place(z, s, yh, x)))
        for z in range(Z)
        for s in range(S)
        for yh in range(YH)
        for x in range(X)
        if keep(z, s, yh, x)
    ]


def move(value, place, keep=lambda z, s, yh, x: True):
    return lax.ppermute(value, AXES, pairs(place, keep))


def along_z(step):
    return lambda z, s, yh, x: (z + step, s, yh, x)


def flip_s(bits):
    return lambda z, s, yh, x: (z, s ^ bits, yh, x)


def first_x(z, s, yh, x):
    return (z, s, yh, x ^ (3 if s % 2 else 1))


def second_x(z, s, yh, x):
    return (z, s, yh, x ^ (1 if s % 2 else 3))


def other_yh(z, s, yh, x):
    return (z, s, 1 - yh, x)


def product(left, right):
    return lax.dot_general(
        left,
        right,
        (((1,), (1,)), ((), ())),
        precision=lax.Precision.HIGH,
        preferred_element_type=jnp.float32,
    )


def pin(value, token):
    corner = value[:8, :128] + 0.0 * token.reshape(-1, token.shape[-1])[:8, :128]
    return lax.dynamic_update_slice(value, corner, (0, 0))


def tie(value, token):
    return value + 0.0 * token[(0,) * token.ndim]


def both(up, down):
    return move(up, along_z(1)), move(down, along_z(-1))


def per_device(jacobian):
    rows = jacobian.shape[0]
    half = rows // 2
    samples = rows * Z * S
    samp, par = lax.axis_index("samp"), lax.axis_index("par")
    z, s, yh, x = samp // S, samp % S, par // X, par % X

    one = both(jacobian, jacobian)
    near = move(jacobian, flip_s(2))
    core = move(jacobian, flip_s(1))

    total = jnp.sum(jacobian, axis=0, keepdims=True)
    totals = jnp.broadcast_to(total, (Z * S, total.shape[1]))
    totals = lax.all_to_all(totals, "samp", 0, 0, tiled=True)
    mean = jnp.sum(totals, axis=0, keepdims=True) / samples

    two = both(*one)
    near = pin(near, one[0][:8] + one[1][:8]) - mean
    near_core = move(near, flip_s(1))
    plane = jnp.stack([jacobian - mean, core - mean, near, near_core])
    second = jnp.where(s % 2 == 0, x ^ 3, x ^ 1)
    left = [
        lax.dynamic_index_in_dim(plane, place ^ s, 0, keepdims=False)
        for place in (x, second, second ^ 2, x ^ 2)
    ]

    def products(blocks, places):
        return jnp.stack(
            [jnp.concatenate([product(left[k], b) for k in places], axis=0) for b in blocks]
        )

    def halve_x(blocks, token=None):
        got = move(products([b - mean for b in blocks], (2, 3)), first_x)
        centre = mean if token is None else tie(mean, token)
        return got, products([b - centre for b in blocks], (0, 1))

    def quarter_x(got, kept):
        kept = kept + got
        return kept[:, :rows], move(kept[:, rows:], second_x)

    got1, kept1 = halve_x((jacobian, *one))
    own1, got1 = quarter_x(got1, kept1)

    two = [pin(b, kept1) for b in two]
    three = both(*two)
    part1 = own1 + got1
    got2, kept2 = halve_x(two, part1)
    part1 = part1 + move(part1, other_yh)
    own2, got2 = quarter_x(got2, kept2)

    far = both(three[0][:half], three[1][half:])
    part2 = own2 + got2
    got3, kept3 = halve_x(three, None)
    part2 = part2 + move(part2, other_yh)
    own3, got3 = quarter_x(got3, kept3)

    far = jnp.concatenate([far[0], far[1]], axis=0)
    part3 = own3 + got3
    got4, kept4 = halve_x([far], None)
    part3 = part3 + move(part3, other_yh)
    own4, got4 = quarter_x(got4, kept4)
    part4 = own4 + got4
    part4 = part4 + move(part4, other_yh)

    done = jnp.stack(
        [part1[0], part1[2], part2[1], part3[1], part4[0], part3[0], part2[0], part1[1]]
    )

    got = []
    for turn in range(X):
        step = (X * yh + (s + turn) % X - z) % Z
        block = lax.dynamic_index_in_dim(done, step, 0, keepdims=False)
        got.append(move(block, lambda z, s, yh, x: (z, x, yh, s + turn)))
    got = jnp.stack(got)
    out = [
        lax.dynamic_index_in_dim(got, (x - m) % X, 0, keepdims=False) for m in range(X)
    ]
    return jnp.concatenate(out, axis=1) / samples


def solution(mesh):
    placed = (P("samp", "par"),)
    return jax.shard_map(
        per_device, mesh=mesh, in_specs=placed, out_specs=P("samp", "par"), check_vma=False
    )
```

```python
import jax
import jax.numpy as jnp
from jax import lax
from jax.sharding import PartitionSpec as P

AXES = ("samp", "par")
Z, S, YH, X = 8, 4, 2, 4


def number(z, s, yh, x):
    return ((z % Z) * S + s) * YH * X + yh * X + x % X


def pairs(place, keep=lambda z, s, yh, x: True):
    return [
        (number(z, s, yh, x), number(*place(z, s, yh, x)))
        for z in range(Z)
        for s in range(S)
        for yh in range(YH)
        for x in range(X)
        if keep(z, s, yh, x)
    ]


def move(value, place, keep=lambda z, s, yh, x: True):
    return lax.ppermute(value, AXES, pairs(place, keep))


def along_z(step):
    return lambda z, s, yh, x: (z + step, s, yh, x)


def flip_s(bits):
    return lambda z, s, yh, x: (z, s ^ bits, yh, x)


def first_x(z, s, yh, x):
    return (z, s, yh, x ^ (3 if s % 2 else 1))


def second_x(z, s, yh, x):
    return (z, s, yh, x ^ (1 if s % 2 else 3))


def other_yh(z, s, yh, x):
    return (z, s, 1 - yh, x)


def product(left, right):
    return lax.dot_general(
        left,
        right,
        (((1,), (1,)), ((), ())),
        precision=lax.Precision.HIGH,
        preferred_element_type=jnp.float32,
    )


def pin(value, token):
    corner = value[:8, :128] + 0.0 * token.reshape(-1, token.shape[-1])[:8, :128]
    return lax.dynamic_update_slice(value, corner, (0, 0))


def tie(value, token):
    return value + 0.0 * token[(0,) * token.ndim]


def both(up, down):
    return move(up, along_z(1)), move(down, along_z(-1))


def per_device(jacobian):
    rows = jacobian.shape[0]
    half = rows // 2
    samples = rows * Z * S
    samp, par = lax.axis_index("samp"), lax.axis_index("par")
    z, s, yh, x = samp // S, samp % S, par // X, par % X

    one = both(jacobian, jacobian)
    near = move(jacobian, flip_s(2))
    core = move(jacobian, flip_s(1))

    total = jnp.sum(jacobian, axis=0, keepdims=True)
    totals = jnp.broadcast_to(total, (Z * S, total.shape[1]))
    totals = lax.all_to_all(totals, "samp", 0, 0, tiled=True)
    mean = jnp.sum(totals, axis=0, keepdims=True) / samples

    two = both(*one)
    near = pin(near, one[0][:8] + one[1][:8]) - mean
    near_core = move(near, flip_s(1))
    plane = jnp.stack([jacobian - mean, core - mean, near, near_core])
    second = jnp.where(s % 2 == 0, x ^ 3, x ^ 1)
    left = [
        lax.dynamic_index_in_dim(plane, place ^ s, 0, keepdims=False)
        for place in (x, second, second ^ 2, x ^ 2)
    ]

    def products(blocks, places):
        return jnp.stack(
            [jnp.concatenate([product(left[k], b) for k in places], axis=0) for b in blocks]
        )

    def halve_x(blocks, token=None):
        got = move(products([b - mean for b in blocks], (2, 3)), first_x)
        centre = mean if token is None else tie(mean, token)
        return got, products([b - centre for b in blocks], (0, 1))

    def quarter_x(got, kept):
        kept = kept + got
        return kept[:, :rows], move(kept[:, rows:], second_x)

    got1, kept1 = halve_x((jacobian, *one))
    own1, got1 = quarter_x(got1, kept1)

    two = [pin(b, kept1) for b in two]
    three = both(*two)
    part1 = own1 + got1
    got2, kept2 = halve_x(two, part1)
    part1 = part1 + move(part1, other_yh)
    own2, got2 = quarter_x(got2, kept2)

    far = both(three[0][:half], three[1][half:])
    part2 = own2 + got2
    got3, kept3 = halve_x(three, part2)
    part2 = part2 + move(part2, other_yh)
    own3, got3 = quarter_x(got3, kept3)

    far = jnp.concatenate([far[0], far[1]], axis=0)
    part3 = own3 + got3
    got4, kept4 = halve_x([far], None)
    part3 = part3 + move(part3, other_yh)
    own4, got4 = quarter_x(got4, kept4)
    part4 = own4 + got4
    part4 = part4 + move(part4, other_yh)

    done = jnp.stack(
        [part1[0], part1[2], part2[1], part3[1], part4[0], part3[0], part2[0], part1[1]]
    )

    got = []
    for turn in range(X):
        step = (X * yh + (s + turn) % X - z) % Z
        block = lax.dynamic_index_in_dim(done, step, 0, keepdims=False)
        got.append(move(block, lambda z, s, yh, x: (z, x, yh, s + turn)))
    got = jnp.stack(got)
    out = [
        lax.dynamic_index_in_dim(got, (x - m) % X, 0, keepdims=False) for m in range(X)
    ]
    return jnp.concatenate(out, axis=1) / samples


def solution(mesh):
    placed = (P("samp", "par"),)
    return jax.shard_map(
        per_device, mesh=mesh, in_specs=placed, out_specs=P("samp", "par"), check_vma=False
    )
```
